32 devices in a mesh: row: 8 (over y, x, core), col: 4 (over z).
Axes of the slice: x: 2, y: 2, z: 4, core: 2. Of those that a mesh axis runs over, the one named last changes fastest.
Arguments:
- source_points: bfloat16 [32768, 1024], P('row'), may hold values from -8 to 8
- target_points: bfloat16 [16384, 1024], P('col', 'row'), may hold values from -8 to 8
- source_mass: float32 [32768], P('row'), may hold values from 0.25 to 4
- target_mass: float32 [16384], P('col'), may hold values from 0.25 to 4
- tile_index: int32 [128, 8], P('row', 'col'), may hold values from 0 to 15, as said below
- tile_count: int32 [128, 4], P('row', 'col'), may hold values from 1 to 2, as said below
Outputs:
- source_potential: float32 [32768], P('row')
- target_potential: float32 [16384], P('col')
The draws below stay inside these ranges and needn't reach their ends.
Inputs may be any that keep to these rules, and one draw needn't show every extreme that they name: `tile_index`: within the 2 slots of one source tile and one index of col the target tiles are distinct; every target tile is named by a live slot of some source tile. `tile_count`: each index of row holds, for every index of col, a source tile with all 2 slots live.
All inputs are finite; a program needn't handle non-finite values.
Results may differ from the reference program's by a relative error of at most 0.0003.
Values may be sent and summed in bfloat16 or wider, within the bound.
No kernel may reach another device: no remote copies, remote signals or barrier semaphores. Data moves between devices by JAX's collectives and lax.ppermute only.
A program may use at most 128 MiB of HBM per device.

```python
import math
import jax
import jax.numpy as jnp
from jax import lax

D = 1024
TILE = 256
KL = 2
ITERS = 3
SR = 4096
TC = 4096
NS = 32768
NT = 16384
RT = 128
CTL = 16
N_COL = 4


def common_direction(key):
    flips = jax.random.bernoulli(jax.random.fold_in(key, 7), 0.5, (D,))
    return jnp.where(flips, 1.0, -1.0).astype(jnp.float32)


def strong_rows(key, base, count, salt):
    chosen = jax.random.bernoulli(jax.random.fold_in(key, salt), 0.125, (count, 1))
    level = jax.random.uniform(jax.random.fold_in(key, salt + 1), (count, 1), jnp.float32, 60.0, 300.0)
    flips = jax.random.bernoulli(jax.random.fold_in(key, salt + 2), 0.5, (count, 1))
    sign = jnp.where(flips, 1.0, -1.0).astype(jnp.float32)
    magnitude = sign * jnp.sqrt(level / math.sqrt(D))
    noise = jax.random.normal(jax.random.fold_in(key, salt + 3), (count, D), jnp.float32)
    strong = magnitude * common_direction(key)[None, :] + 0.3 * noise
    return jnp.where(chosen, strong, base)


def draw_source_points(key, part):
    noise = jax.random.normal(jax.random.fold_in(key, 1), (NS, D), jnp.float32)
    base = noise
    values = strong_rows(key, base, NS, 21)
    return jnp.clip(values, -8.0, 8.0).astype(jnp.bfloat16)


def draw_target_points(key, part):
    noise = jax.random.normal(jax.random.fold_in(key, 3), (NT, D), jnp.float32)
    base = noise
    values = strong_rows(key, base, NT, 31)
    return jnp.clip(values, -8.0, 8.0).astype(jnp.bfloat16)


def draw_tile_index(key, part):
    groups = RT * N_COL
    keys = jax.random.split(jax.random.fold_in(key, 11), groups)
    perms = jax.vmap(lambda one: jax.random.permutation(one, CTL))(keys).astype(jnp.int32)
    rows = jnp.arange(groups) // N_COL
    cols = jnp.arange(groups) % N_COL
    shifts = jax.random.randint(jax.random.fold_in(key, 12), (N_COL,), 0, CTL)
    target = ((rows + shifts[cols]) % CTL).astype(jnp.int32)
    rest = jnp.where(perms[:, 1:] == target[:, None], perms[:, :1], perms[:, 1:])
    listed = jnp.concatenate([target[:, None], rest], axis=1)[:, :KL]
    return listed.reshape(RT, N_COL * KL).astype(jnp.int32)


def draw_tile_count(key, part):
    counts = jax.random.randint(jax.random.fold_in(key, 13), (RT, N_COL), 1, KL + 1)
    picks = jax.random.randint(jax.random.fold_in(key, 14), (N_COL,), 0, SR // TILE)
    forced = jnp.arange(RT)[:, None] % (SR // TILE) == picks[None, :]
    return jnp.where(forced, KL, counts).astype(jnp.int32)


def block_scale(rng, dims, shards, least, top_value):
    def one(axis_at, blocks):
        draws = jax.random.uniform(jax.random.fold_in(jax.random.fold_in(rng, 6), axis_at), (blocks,), jnp.float32, least / len(shards), top_value / len(shards))
        return jnp.repeat(jnp.exp(draws), dims[axis_at] // blocks).reshape((-1,) + (1,) * (len(dims) - axis_at - 1))

    gain = one(*shards[0])
    for cut in shards[1:]:
        gain = gain * one(*cut)
    return gain


def setup_inputs(seed: int = 0) -> dict:
    key_list = jax.random.split(jax.random.key(seed), 7)
    return {
        "source_points": draw_source_points(jax.random.fold_in(key_list[6], 71), 0),
        "target_points": draw_target_points(jax.random.fold_in(key_list[6], 71), 0),
        "source_mass": jnp.clip(jnp.exp(math.log(4.0) - 2.7725887 * jax.random.uniform(key_list[2], (NS,), jnp.float32) ** block_scale(key_list[2], (NS,), ((0, 8),), -0.2, 0.2)), 0.25, 4.0),
        "target_mass": jnp.clip(jnp.exp(math.log(4.0) - 2.7725887 * jax.random.uniform(key_list[3], (NT,), jnp.float32) ** block_scale(key_list[3], (NT,), ((0, 4),), -0.2, 0.2)), 0.25, 4.0),
        "tile_index": draw_tile_index(jax.random.fold_in(key_list[6], 71), 0),
        "tile_count": draw_tile_count(jax.random.fold_in(key_list[6], 71), 0),
    }


def reference(source_points, target_points, source_mass, target_mass, tile_index, tile_count):
    masked_score = -1e+30
    col_tiles = TC // TILE
    total_tiles = NT // TILE
    slots = N_COL * KL
    offsets = (jnp.arange(slots) // KL * col_tiles).astype(jnp.int32)
    global_index = (tile_index + offsets[None, :]).astype(jnp.int32)
    live = (jnp.arange(slots) % KL)[None, :] < jnp.repeat(tile_count, KL, axis=1)
    target_tiles = target_points.reshape(total_tiles, TILE, D)
    source_tiles = source_points.reshape(RT, TILE, D)
    log_source = jnp.log(source_mass).reshape(RT, TILE)
    log_target = jnp.log(target_mass).reshape(total_tiles, TILE)
    scale = 1.0 / math.sqrt(D)
    target_pot = jnp.zeros((total_tiles, TILE), jnp.float32)
    row_pots = None
    for iteration in range(ITERS):

        def visit(carry, inputs, target_pot=target_pot):
            col_top, col_sum = carry
            rows, chosen, alive, log_row = inputs
            cost = jnp.einsum('ad,sbd->sab', rows.astype(jnp.float32), target_tiles[chosen].astype(jnp.float32), precision=lax.Precision.HIGHEST) * scale
            scores = jnp.where(alive[:, None, None], cost + target_pot[chosen][:, None, :], masked_score)
            top = lax.optimization_barrier(jnp.max(scores, axis=(0, 2)))
            total = lax.optimization_barrier(jnp.sum(jnp.exp(scores - top[None, :, None]), axis=(0, 2)))
            row_pot = log_row - top - jnp.log(total)
            columns = jnp.where(alive[:, None, None], cost + row_pot[None, :, None], masked_score)
            slot_top = lax.optimization_barrier(jnp.max(columns, axis=1))
            old_top = col_top[chosen]
            new_top = jnp.maximum(old_top, slot_top)
            sums = lax.optimization_barrier(jnp.sum(jnp.exp(columns - new_top[:, None, :]), axis=1))
            sums = jnp.where(alive[:, None], sums, 0.0)
            new_sum = col_sum[chosen] * jnp.exp(old_top - new_top) + sums
            col_top = col_top.at[chosen].set(new_top)
            col_sum = col_sum.at[chosen].set(new_sum)
            return ((col_top, col_sum), row_pot)
        start = (jnp.full((total_tiles, TILE), masked_score, jnp.float32), jnp.zeros((total_tiles, TILE), jnp.float32))
        (col_top, col_sum), row_pots = lax.scan(visit, start, (source_tiles, global_index, live, log_source))
        target_pot = log_target - col_top - jnp.log(col_sum)
    return (row_pots.reshape(-1), target_pot.reshape(-1))
```

```python
import functools
import math

import jax
import jax.numpy as jnp
from jax import lax
from jax.experimental import pallas as pl
from jax.experimental.pallas import tpu as pltpu
from jax.sharding import PartitionSpec as P

TILE = 256
LANES = 128
STRIP = 32
HALF = 64
LOW = -1e30
FLOOR = -1e29
LEAST = 1e-15
LOG2_E = math.log2(math.e)
LN_2 = math.log(2.0)

VMEM = pltpu.MemorySpace.VMEM
SMEM = pltpu.MemorySpace.SMEM
NT = (((1,), (1,)), ((), ()))


def kernel_call(body, outs, operands, scratch, name, final=False, aliases=None):
    specs = []
    placed = []
    for x in operands:
        if x.dtype == jnp.int32:
            specs.append(pl.BlockSpec(memory_space=SMEM))
            placed.append(x)
        else:
            specs.append(pl.BlockSpec(memory_space=VMEM))
            placed.append(pltpu.with_memory_space_constraint(x, VMEM))
    return pl.pallas_call(
        body,
        out_shape=[
            (jax.ShapeDtypeStruct if final else VMEM)(shape, jnp.float32) for shape in outs
        ],
        in_specs=specs,
        out_specs=[pl.BlockSpec(memory_space=VMEM)] * len(outs),
        input_output_aliases=aliases or {},
        scratch_shapes=[pltpu.VMEM(shape, jnp.float32) for shape in scratch],
        cost_estimate=pl.CostEstimate(flops=1 << 13, bytes_accessed=1 << 10, transcendentals=0),
        compiler_params=pltpu.CompilerParams(vmem_limit_bytes=8 << 20),
        name=name,
    )(*placed)


def to_rows(columns, tiles):
    return columns.T[:tiles]


def to_columns(rows):
    tiles = rows.shape[0]
    padded = jnp.concatenate([rows, jnp.zeros((LANES - tiles, TILE), jnp.float32)], axis=0)
    return padded.T


def put_lanes(ref, start, columns):
    rows = pl.ds(start, STRIP)
    lane = lax.broadcasted_iota(jnp.int32, (STRIP, LANES), 1)
    value = ref[rows, :]
    for at, column in columns.items():
        value = jnp.where(lane == at, column, value)
    ref[rows, :] = value


def halves(x, op):
    return op(x[:, :LANES], x[:, LANES:])


def from_flat(ref):
    step = TILE // LANES
    parts = [ref[pl.ds(h, ref.shape[0] // step, stride=step), :] for h in range(step)]
    return jnp.concatenate(parts, axis=1)


def put_flat(ref, value):
    for h in range(TILE // LANES):
        ref[pl.ds(h, value.shape[0], stride=TILE // LANES), :] = value[:, h * LANES : (h + 1) * LANES]


def score_kernel(distances, first, last, scale, *refs):
    pieces = len(distances)
    index, count, source = refs[:3]
    targets = refs[3 : 3 + pieces]
    refs = refs[3 + pieces :]
    if not first:
        before, *refs = refs
    score, *outs, columns = refs
    tiles, slots = score.shape[:2]
    me = lax.axis_index("row")
    offset = [
        (me ^ jnp.where((me & 1) == 0, zero, one)) * target.shape[1]
        for (zero, one), target in zip(distances, targets)
    ]
    if targets[0].shape[1] == source.shape[1]:
        offset = [0]
    if first:
        name_slots(index, count, outs[-1], slots)

    def products(t):
        rows = pl.ds(t * TILE if last else pl.multiple_of(t * TILE, TILE), TILE)
        left = [
            source[rows, pl.ds(pl.multiple_of(offset[k], targets[k].shape[1]), targets[k].shape[1])]
            for k in range(pieces)
        ]
        left = jnp.concatenate(left, axis=1) if pieces > 1 else left[0]
        for s in range(slots):
            chosen = pl.ds(pl.multiple_of(index[s, t] * TILE, TILE), TILE)
            right = [targets[k][chosen, :] for k in range(pieces)]
            right = jnp.concatenate(right, axis=1) if pieces > 1 else right[0]
            block = lax.dot_general(left, right, NT, preferred_element_type=jnp.float32)
            if not first:
                block = before[t, s] + block
            if last:
                block = block * scale
                if s > 0:
                    block = jnp.where(s < count[0, t], block, LOW)
            score[t, s] = block

    def statistics(t):
        for r in range(0, TILE, STRIP):
            blocks = [score[t, s, r : r + STRIP] for s in range(slots)]
            top = halves(functools.reduce(jnp.maximum, blocks), jnp.maximum)
            top = jnp.max(top, axis=1, keepdims=True)
            total = functools.reduce(jnp.add, [jnp.exp2(block - top) for block in blocks])
            total = jnp.sum(halves(total, jnp.add), axis=1, keepdims=True)
            put_lanes(columns, r, {t: top, HALF + t: total})

    if last:
        for t in range(tiles + 1):
            if t < tiles:
                products(t)
            if t > 0:
                statistics(t - 1)
        stats = columns[...].T
        outs[0][0] = stats[:tiles]
        outs[0][1] = stats[HALF : HALF + tiles]
    else:
        lax.fori_loop(0, tiles, lambda t, carry: (products(t), carry)[1], 0, unroll=4)
    if not first and not last:
        outs[0][...] = jnp.zeros(outs[0].shape, jnp.float32)


def name_slots(index, count, names, slots):
    for k in range(names.shape[0]):
        t, s = divmod(k, slots)
        name = jnp.where(s < count[0, t], index[s, t], -1).astype(jnp.float32)
        names[k : k + 1, :] = jnp.full((1, TILE), name, jnp.float32)


def to_slots(names, rows):
    taken = jnp.zeros(names.shape, jnp.float32)
    for u in range(rows.shape[0]):
        taken = jnp.where(names == u, rows[u : u + 1, :], taken)
    return taken


def to_targets(names, values, out, op, empty):
    for u in range(out.shape[0]):
        out[u : u + 1, :] = op(jnp.where(names == u, values, empty), axis=0, keepdims=True)


def merge(refs):
    top = functools.reduce(jnp.maximum, [ref[0] for ref in refs])
    total = functools.reduce(jnp.add, [ref[1] * jnp.exp2(ref[0] - top) for ref in refs])
    return top, total


def total_of(refs):
    return functools.reduce(jnp.add, [ref[...] for ref in refs])


def exp_kernel(score, stats, kernel, columns):
    tiles, slots = kernel.shape[:2]
    columns[...] = to_columns(stats[0])
    for t in range(tiles):
        for r in range(0, TILE, STRIP):
            column = columns[r : r + STRIP, t : t + 1]
            for s in range(slots):
                kernel[t, s, r : r + STRIP] = jnp.exp2(score[t, s, r : r + STRIP] - column)


def slot_sums(kernel, columns, sums):
    tiles, slots = kernel.shape[:2]
    for t in range(tiles):
        total = [None] * slots
        for r in range(0, TILE, STRIP):
            column = columns[r : r + STRIP, t : t + 1]
            for s in range(slots):
                block = kernel[t, s, r : r + STRIP] * column
                total[s] = block if r == 0 else total[s] + block
        for s in range(slots):
            k = t * slots + s
            sums[k : k + 1, :] = jnp.sum(total[s], axis=0, keepdims=True)


def first_column_kernel(parts, names, score, before, mass, *refs):
    gathered = refs[:parts]
    kernel, stats, tops, potential, factor, columns, sums = refs[parts:]
    tiles, slots = kernel.shape[:2]
    top, total = merge(gathered)
    row = LOG2_E * (jnp.log(from_flat(mass)) - jnp.log(total)) - top
    potential[...] = row
    factor[...] = jnp.exp2(gathered[0][0] + row)
    columns[...] = to_columns(factor[...])
    slot_sums(before, columns, sums)
    tops[...] = jnp.zeros(tops.shape, jnp.float32)
    least = jnp.min(jnp.where(names[...] >= 0, sums[...], 1.0))

    @pl.when(least < LEAST)
    def _():
        factor[...] = jnp.ones(factor.shape, jnp.float32)
        columns[...] = to_columns(row)
        for t in range(tiles):
            best = [None] * slots
            for r in range(0, TILE, STRIP):
                column = columns[r : r + STRIP, t : t + 1]
                for s in range(slots):
                    block = score[t, s, r : r + STRIP] + column
                    best[s] = block if r == 0 else jnp.maximum(best[s], block)
            best = [jnp.maximum(jnp.max(x, axis=0, keepdims=True), FLOOR) for x in best]
            total = [None] * slots
            for r in range(0, TILE, STRIP):
                column = columns[r : r + STRIP, t : t + 1]
                for s in range(slots):
                    block = jnp.exp2(score[t, s, r : r + STRIP] + column - best[s])
                    kernel[t, s, r : r + STRIP] = block
                    total[s] = block if r == 0 else total[s] + block
            for s in range(slots):
                k = t * slots + s
                tops[k : k + 1, :] = best[s]
                sums[k : k + 1, :] = jnp.sum(total[s], axis=0, keepdims=True)

    named = names[...]
    to_targets(named, tops[...], stats.at[0], jnp.max, FLOOR)
    change = jnp.exp2(tops[...] - to_slots(named, stats[0]))
    to_targets(named, sums[...] * change, stats.at[1], jnp.sum, 0.0)


def row_sums(kernel, weights, factor, out, columns):
    tiles, slots = kernel.shape[:2]
    for t in range(tiles):
        weight = [weights[t * slots + s : t * slots + s + 1, :] for s in range(slots)]
        for r in range(0, TILE, STRIP):
            blocks = [kernel[t, s, r : r + STRIP] * weight[s] for s in range(slots)]
            total = halves(functools.reduce(jnp.add, blocks), jnp.add)
            put_lanes(columns, r, {t: jnp.sum(total, axis=1, keepdims=True)})
    out[...] = to_rows(columns[...], tiles) * factor[...]


def first_row_kernel(parts, names, kernel, mass, factor, tops, *refs):
    gathered = refs[:parts]
    out, potential, weights, columns = refs[parts:]
    top, total = merge(gathered)
    value = LOG2_E * (jnp.log(from_flat(mass)) - jnp.log(total)) - top
    potential[...] = value
    weights[...] = jnp.exp2(tops[...] + to_slots(names[...], value))
    row_sums(kernel, weights, factor, out, columns)


def column_kernel(parts, last, names, kernel, mass, factor, weights, *refs):
    if last:
        start, *refs = refs
    gathered = refs[:parts]
    out, *potential, columns, sums = refs[parts:]
    scaling = from_flat(mass) / total_of(gathered)
    columns[...] = to_columns(scaling * factor[...])
    slot_sums(kernel, columns, sums)
    to_targets(names[...], sums[...] * weights[...], out, jnp.sum, 0.0)
    if last:
        put_flat(potential[0], LN_2 * start[...] + jnp.log(scaling))


def row_kernel(parts, names, kernel, mass, factor, weights, *refs):
    gathered = refs[:parts]
    out, columns, scaled = refs[parts:]
    scaling = from_flat(mass) / total_of(gathered)
    scaled[...] = weights[...] * to_slots(names[...], scaling)
    row_sums(kernel, scaled, factor, out, columns)


def last_kernel(parts, mass, start, *refs):
    scaling = from_flat(mass) / total_of(refs[:parts])
    put_flat(refs[parts], LN_2 * start[...] + jnp.log(scaling))


def permute(x, axis, n, partner):
    return lax.ppermute(x, axis, [(i, partner(i)) for i in range(n)])


def swap(x, axis, n, mask):
    return permute(x, axis, n, lambda i: i ^ mask)


def merged(pairs):
    top = functools.reduce(jnp.maximum, [pair[0] for pair in pairs])
    total = functools.reduce(jnp.add, [pair[1] * jnp.exp2(pair[0] - top) for pair in pairs])
    here = lax.broadcasted_iota(jnp.int32, pairs[0].shape, 0)
    return jnp.where(here == 0, top[None], total[None])


def exchange(x, axis, sizes, join, orders=((3, 1), (2, 3), (1, 2))):
    n_row, n_col = sizes
    n = n_row if axis == "row" else n_col
    if n & (n - 1):
        return [lax.all_gather(x, axis)[k] for k in range(n)]
    low = 1
    while n // low not in (1, 4):
        x = join([x, swap(x, axis, n, low)])
        low *= 2
    if low == n:
        return [x]
    mixed = axis == "col" or low > 1
    parts = [x]
    for even, odd in orders:
        pairs = []
        for row in range(n_row):
            for col in range(n_col):
                mask = low * (odd if mixed and row & 1 else even)
                to = (row ^ mask, col) if axis == "row" else (row, col ^ mask)
                pairs.append((row * n_col + col, to[0] * n_col + to[1]))
        parts.append(lax.ppermute(x, ("row", "col"), pairs))
    return parts


def first_way(i):
    return i ^ (4 if i & 1 else 2)


def second_way(i):
    return i ^ (2 if i & 1 else 4)


def scores_by_chip(score, target, n):
    first = permute(target, "row", n, first_way)
    part, names = score(None, [(target, (0, 0))], False)
    later, names = lax.optimization_barrier((target, names))
    second = permute(later, "row", n, second_way)
    first, part, names = lax.optimization_barrier((first, part, names))
    half = first.shape[0] // 2
    early, late = (permute(part, "row", n, second_way) for part in (first[:half], first[half:]))
    sibling = swap(target, "row", n, 1)
    first_sibling = swap(first, "row", n, 1)
    part, second = lax.optimization_barrier((part, second))
    pieces = [(sibling, (1, 1)), (first, (2, 4)), (first_sibling, (5, 3))]
    part, mark = score(part, pieces, False)
    second, early, part, _ = lax.optimization_barrier((second, early, part, mark))
    second_sibling = swap(second, "row", n, 1)
    early_sibling = swap(early, "row", n, 1)
    late, early_sibling = lax.optimization_barrier((late, early_sibling))
    corner = jnp.concatenate([early, late], axis=0)
    corner_sibling = jnp.concatenate([early_sibling, swap(late, "row", n, 1)], axis=0)
    pieces = [(second, (4, 2)), (second_sibling, (3, 5)), (corner, (6, 6)), (corner_sibling, (7, 7))]
    return [*score(part, pieces, True), names]


def on_device(n_row, n_col, source, target, source_mass, target_mass, tile_index, tile_count):
    tiles = source.shape[0] // TILE
    col_tiles = target.shape[0] // TILE
    slots = tile_index.shape[1]
    scale = LOG2_E / math.sqrt(source.shape[1])
    pairs = tiles * slots * TILE * TILE
    grid = (tiles, slots, TILE, TILE)
    source_rows, target_rows = (tiles, TILE), (col_tiles, TILE)
    a = source_mass.reshape(-1, LANES)
    b = target_mass.reshape(-1, LANES)
    index, count = tile_index.T, tile_count.T
    slot_rows = (tiles * slots, TILE)
    columns = (TILE, LANES)
    sizes = (n_row, n_col)

    def score(before, pieces, last):
        operands = [index, count, source, *[piece for piece, _ in pieces]]
        outs = [grid]
        if last:
            outs.append((2, *source_rows))
        if before is None:
            outs.append(slot_rows)
        else:
            operands.append(before)
            if not last:
                outs.append((8, LANES))
        distances = [k for _, k in pieces]
        return kernel_call(
            functools.partial(score_kernel, distances, before is None, last, scale),
            outs,
            operands,
            [columns],
            f"score_{len(pieces)}_{last}",
        )

    if n_row == 8 and target.shape[1] % LANES == 0:
        scores, stats, names = scores_by_chip(score, target, n_row)
    else:
        whole = lax.all_gather(target, "row", axis=1, tiled=True)
        scores, stats, names = score(None, [(whole, (0, 0))], True)

    def phase(body, name, outs, operands, parts, scratch=(), final=False, aliases=None):
        body = functools.partial(body, len(parts))
        return kernel_call(body, outs, [*operands, *parts], scratch, name, final, aliases)

    def added(values):
        return functools.reduce(jnp.add, values)

    flat = (tiles * TILE // LANES, LANES)
    parts = exchange(stats, "col", sizes, merged, ((1, 2), (3, 1), (2, 3)))
    (kernel,) = kernel_call(exp_kernel, [grid], [scores, stats], [columns], "exps")
    kernel, stats, tops, f_first, factor = phase(
        first_column_kernel,
        "column_0",
        [grid, (2, *target_rows), slot_rows, source_rows, source_rows],
        [names, scores, kernel, a],
        parts,
        [columns, slot_rows],
        aliases={2: 0},
    )
    parts = exchange(stats, "row", sizes, merged)
    sums, g_first, weights = phase(
        first_row_kernel,
        "row_1",
        [source_rows, target_rows, slot_rows],
        [names, kernel, b, factor, tops],
        parts,
        [columns],
    )
    parts = exchange(sums, "col", sizes, added)
    (sums,) = phase(
        lambda n, *refs: column_kernel(n, False, *refs),
        "column_1",
        [target_rows],
        [names, kernel, a, factor, weights],
        parts,
        [columns, slot_rows],
    )
    parts = exchange(sums, "row", sizes, added)
    (sums,) = phase(
        row_kernel,
        "row_2",
        [source_rows],
        [names, kernel, b, factor, weights],
        parts,
        [columns, slot_rows],
    )
    parts = exchange(sums, "col", sizes, added)
    sums, f_last = phase(
        lambda n, *refs: column_kernel(n, True, *refs),
        "column_2",
        [target_rows, flat],
        [names, kernel, a, factor, weights, f_first],
        parts,
        [columns, slot_rows],
    )
    parts = exchange(sums, "row", sizes, added)
    (g_last,) = phase(
        last_kernel, "last", [(col_tiles * TILE // LANES, LANES)], [b, g_first], parts, final=True
    )
    return (f_last.reshape(-1), g_last.reshape(-1))


def solution(mesh):
    placed = (P("row", None), P("col", "row"), P("row"), P("col"), P("row", "col"), P("row", "col"))
    return jax.shard_map(
        functools.partial(on_device, mesh.shape["row"], mesh.shape["col"]),
        mesh=mesh,
        in_specs=placed,
        out_specs=(P("row"), P("col")),
        check_vma=False,
    )
```

```python
import functools
import math

import jax
import jax.numpy as jnp
from jax import lax
from jax.experimental import pallas as pl
from jax.experimental.pallas import tpu as pltpu
from jax.sharding import PartitionSpec as P

TILE = 256
LANES = 128
STRIP = 32
FINE = 16
HALF = 64
LOW = -1e30
FLOOR = -1e29
LEAST = 1e-15
LOG2_E = math.log2(math.e)
LN_2 = math.log(2.0)

VMEM = pltpu.MemorySpace.VMEM
SMEM = pltpu.MemorySpace.SMEM
NT = (((1,), (1,)), ((), ()))


def kernel_call(body, outs, operands, scratch, name, final=False, aliases=None):
    specs = []
    placed = []
    for x in operands:
        if x.dtype == jnp.int32:
            specs.append(pl.BlockSpec(memory_space=SMEM))
            placed.append(x)
        else:
            specs.append(pl.BlockSpec(memory_space=VMEM))
            placed.append(pltpu.with_memory_space_constraint(x, VMEM))
    return pl.pallas_call(
        body,
        out_shape=[
            (jax.ShapeDtypeStruct if final else VMEM)(shape, jnp.float32) for shape in outs
        ],
        in_specs=specs,
        out_specs=[pl.BlockSpec(memory_space=VMEM)] * len(outs),
        input_output_aliases=aliases or {},
        scratch_shapes=[pltpu.VMEM(shape, jnp.float32) for shape in scratch],
        cost_estimate=pl.CostEstimate(flops=1 << 13, bytes_accessed=1 << 10, transcendentals=0),
        compiler_params=pltpu.CompilerParams(vmem_limit_bytes=8 << 20),
        name=name,
    )(*placed)


def to_rows(columns, tiles):
    return columns.T[:tiles]


def to_columns(rows):
    tiles = rows.shape[0]
    padded = jnp.concatenate([rows, jnp.zeros((LANES - tiles, TILE), jnp.float32)], axis=0)
    return padded.T


def put_lanes(ref, start, columns):
    size = next(iter(columns.values())).shape[0]
    rows = pl.ds(start, size)
    lane = lax.broadcasted_iota(jnp.int32, (size, LANES), 1)
    value = ref[rows, :]
    for at, column in columns.items():
        value = jnp.where(lane == at, column, value)
    ref[rows, :] = value


def halves(x, op):
    return op(x[:, :LANES], x[:, LANES:])


def from_flat(ref):
    step = TILE // LANES
    parts = [ref[pl.ds(h, ref.shape[0] // step, stride=step), :] for h in range(step)]
    return jnp.concatenate(parts, axis=1)


def put_flat(ref, value):
    for h in range(TILE // LANES):
        ref[pl.ds(h, value.shape[0], stride=TILE // LANES), :] = value[:, h * LANES : (h + 1) * LANES]


def score_kernel(distances, first, last, scale, *refs):
    pieces = len(distances)
    index, count, source = refs[:3]
    targets = refs[3 : 3 + pieces]
    refs = refs[3 + pieces :]
    if not first:
        before, *refs = refs
    score, *outs, columns = refs
    tiles, slots = score.shape[:2]
    me = lax.axis_index("row")
    offset = [
        (me ^ jnp.where((me & 1) == 0, zero, one)) * target.shape[1]
        for (zero, one), target in zip(distances, targets)
    ]
    if targets[0].shape[1] == source.shape[1]:
        offset = [0]
    if first:
        name_slots(index, count, outs[-1], slots)

    def products(t):
        rows = pl.ds(t * TILE if last else pl.multiple_of(t * TILE, TILE), TILE)
        left = [
            source[rows, pl.ds(pl.multiple_of(offset[k], targets[k].shape[1]), targets[k].shape[1])]
            for k in range(pieces)
        ]
        left = jnp.concatenate(left, axis=1) if pieces > 1 else left[0]
        for s in range(slots):
            chosen = pl.ds(pl.multiple_of(index[s, t] * TILE, TILE), TILE)
            right = [targets[k][chosen, :] for k in range(pieces)]
            right = jnp.concatenate(right, axis=1) if pieces > 1 else right[0]
            block = lax.dot_general(left, right, NT, preferred_element_type=jnp.float32)
            if not first:
                block = before[t, s] + block
            if last:
                block = block * scale
                if s > 0:
                    block = jnp.where(s < count[0, t], block, LOW)
            score[t, s] = block

    def statistics(t):
        for r in range(0, TILE, FINE):
            blocks = [score[t, s, r : r + FINE] for s in range(slots)]
            top = halves(functools.reduce(jnp.maximum, blocks), jnp.maximum)
            top = jnp.max(top, axis=1, keepdims=True)
            total = functools.reduce(jnp.add, [jnp.exp2(block - top) for block in blocks])
            total = jnp.sum(halves(total, jnp.add), axis=1, keepdims=True)
            put_lanes(columns, r, {t: top, HALF + t: total})

    if last:
        for t in range(tiles + 1):
            if t < tiles:
                products(t)
            if t > 0:
                statistics(t - 1)
        stats = columns[...].T
        outs[0][0] = stats[:tiles]
        outs[0][1] = stats[HALF : HALF + tiles]
    else:
        lax.fori_loop(0, tiles, lambda t, carry: (products(t), carry)[1], 0, unroll=4)
    if not first and not last:
        outs[0][...] = jnp.zeros(outs[0].shape, jnp.float32)


def name_slots(index, count, names, slots):
    for k in range(names.shape[0]):
        t, s = divmod(k, slots)
        name = jnp.where(s < count[0, t], index[s, t], -1).astype(jnp.float32)
        names[k : k + 1, :] = jnp.full((1, TILE), name, jnp.float32)


def to_slots(names, rows):
    taken = jnp.zeros(names.shape, jnp.float32)
    for u in range(rows.shape[0]):
        taken = jnp.where(names == u, rows[u : u + 1, :], taken)
    return taken


def to_targets(names, values, out, op, empty):
    for u in range(out.shape[0]):
        out[u : u + 1, :] = op(jnp.where(names == u, values, empty), axis=0, keepdims=True)


def merge(refs):
    top = functools.reduce(jnp.maximum, [ref[0] for ref in refs])
    total = functools.reduce(jnp.add, [ref[1] * jnp.exp2(ref[0] - top) for ref in refs])
    return top, total


def total_of(refs):
    return functools.reduce(jnp.add, [ref[...] for ref in refs])


def exp_kernel(score, stats, kernel, columns):
    tiles, slots = kernel.shape[:2]
    columns[...] = to_columns(stats[0])
    for t in range(tiles):
        for r in range(0, TILE, STRIP):
            column = columns[r : r + STRIP, t : t + 1]
            for s in range(slots):
                kernel[t, s, r : r + STRIP] = jnp.exp2(score[t, s, r : r + STRIP] - column)


def slot_sums(kernel, columns, sums):
    tiles, slots = kernel.shape[:2]
    for t in range(tiles):
        total = [None] * slots
        for r in range(0, TILE, STRIP):
            column = columns[r : r + STRIP, t : t + 1]
            for s in range(slots):
                block = kernel[t, s, r : r + STRIP] * column
                total[s] = block if r == 0 else total[s] + block
        for s in range(slots):
            k = t * slots + s
            sums[k : k + 1, :] = jnp.sum(total[s], axis=0, keepdims=True)


def first_column_kernel(parts, names, score, before, mass, *refs):
    gathered = refs[:parts]
    kernel, stats, tops, potential, factor, columns, sums = refs[parts:]
    tiles, slots = kernel.shape[:2]
    top, total = merge(gathered)
    row = LOG2_E * (jnp.log(from_flat(mass)) - jnp.log(total)) - top
    potential[...] = row
    factor[...] = jnp.exp2(gathered[0][0] + row)
    columns[...] = to_columns(factor[...])
    slot_sums(before, columns, sums)
    named = names[...]
    tops[...] = jnp.zeros(tops.shape, jnp.float32)
    to_targets(named, sums[...], stats.at[1], jnp.sum, 0.0)
    stats[0] = jnp.where(stats[1] > 0.0, 0.0, FLOOR)
    least = jnp.min(jnp.where(named >= 0, sums[...], 1.0))

    @pl.when(least < LEAST)
    def _():
        factor[...] = jnp.ones(factor.shape, jnp.float32)
        columns[...] = to_columns(row)
        for t in range(tiles):
            best = [None] * slots
            for r in range(0, TILE, STRIP):
                column = columns[r : r + STRIP, t : t + 1]
                for s in range(slots):
                    block = score[t, s, r : r + STRIP] + column
                    best[s] = block if r == 0 else jnp.maximum(best[s], block)
            best = [jnp.maximum(jnp.max(x, axis=0, keepdims=True), FLOOR) for x in best]
            total = [None] * slots
            for r in range(0, TILE, STRIP):
                column = columns[r : r + STRIP, t : t + 1]
                for s in range(slots):
                    block = jnp.exp2(score[t, s, r : r + STRIP] + column - best[s])
                    kernel[t, s, r : r + STRIP] = block
                    total[s] = block if r == 0 else total[s] + block
            for s in range(slots):
                k = t * slots + s
                tops[k : k + 1, :] = best[s]
                sums[k : k + 1, :] = jnp.sum(total[s], axis=0, keepdims=True)
        to_targets(named, tops[...], stats.at[0], jnp.max, FLOOR)
        change = jnp.exp2(tops[...] - to_slots(named, stats[0]))
        to_targets(named, sums[...] * change, stats.at[1], jnp.sum, 0.0)


def row_sums(kernel, weights, factor, out, columns):
    tiles, slots = kernel.shape[:2]
    for t in range(tiles):
        weight = [weights[t * slots + s : t * slots + s + 1, :] for s in range(slots)]
        for r in range(0, TILE, STRIP):
            blocks = [kernel[t, s, r : r + STRIP] * weight[s] for s in range(slots)]
            total = halves(functools.reduce(jnp.add, blocks), jnp.add)
            put_lanes(columns, r, {t: jnp.sum(total, axis=1, keepdims=True)})
    out[...] = to_rows(columns[...], tiles) * factor[...]


def first_row_kernel(parts, names, kernel, mass, factor, tops, *refs):
    gathered = refs[:parts]
    out, potential, weights, columns = refs[parts:]
    top, total = merge(gathered)
    value = LOG2_E * (jnp.log(from_flat(mass)) - jnp.log(total)) - top
    potential[...] = value
    weights[...] = jnp.exp2(tops[...] + to_slots(names[...], value))
    row_sums(kernel, weights, factor, out, columns)


def column_kernel(parts, last, names, kernel, mass, factor, weights, *refs):
    if last:
        start, *refs = refs
    gathered = refs[:parts]
    out, *potential, columns, sums = refs[parts:]
    scaling = from_flat(mass) / total_of(gathered)
    columns[...] = to_columns(scaling * factor[...])
    slot_sums(kernel, columns, sums)
    to_targets(names[...], sums[...] * weights[...], out, jnp.sum, 0.0)
    if last:
        put_flat(potential[0], LN_2 * start[...] + jnp.log(scaling))


def row_kernel(parts, names, kernel, mass, factor, weights, *refs):
    gathered = refs[:parts]
    out, columns, scaled = refs[parts:]
    scaling = from_flat(mass) / total_of(gathered)
    scaled[...] = weights[...] * to_slots(names[...], scaling)
    row_sums(kernel, scaled, factor, out, columns)


def last_kernel(parts, mass, start, *refs):
    scaling = from_flat(mass) / total_of(refs[:parts])
    put_flat(refs[parts], LN_2 * start[...] + jnp.log(scaling))


def permute(x, axis, n, partner):
    return lax.ppermute(x, axis, [(i, partner(i)) for i in range(n)])


def swap(x, axis, n, mask):
    return permute(x, axis, n, lambda i: i ^ mask)


def merged(pairs):
    top = functools.reduce(jnp.maximum, [pair[0] for pair in pairs])
    total = functools.reduce(jnp.add, [pair[1] * jnp.exp2(pair[0] - top) for pair in pairs])
    here = lax.broadcasted_iota(jnp.int32, pairs[0].shape, 0)
    return jnp.where(here == 0, top[None], total[None])


def exchange(x, axis, sizes, join, orders=((3, 1), (2, 3), (1, 2))):
    n_row, n_col = sizes
    n = n_row if axis == "row" else n_col
    if n & (n - 1):
        return [lax.all_gather(x, axis)[k] for k in range(n)]
    low = 1
    while n // low not in (1, 4):
        x = join([x, swap(x, axis, n, low)])
        low *= 2
    if low == n:
        return [x]
    mixed = axis == "col" or low > 1
    parts = [x]
    for even, odd in orders:
        pairs = []
        for row in range(n_row):
            for col in range(n_col):
                mask = low * (odd if mixed and row & 1 else even)
                to = (row ^ mask, col) if axis == "row" else (row, col ^ mask)
                pairs.append((row * n_col + col, to[0] * n_col + to[1]))
        parts.append(lax.ppermute(x, ("row", "col"), pairs))
    return parts


def first_way(i):
    return i ^ (4 if i & 1 else 2)


def second_way(i):
    return i ^ (2 if i & 1 else 4)


def scores_by_chip(score, target, n):
    first = permute(target, "row", n, first_way)
    part, names = score(None, [(target, (0, 0))], False)
    later, names = lax.optimization_barrier((target, names))
    second = permute(later, "row", n, second_way)
    first, part, names = lax.optimization_barrier((first, part, names))
    cut = first.shape[0] // 2
    early, late = (permute(part, "row", n, second_way) for part in (first[:cut], first[cut:]))
    sibling = swap(target, "row", n, 1)
    first_sibling = swap(first, "row", n, 1)
    part, second = lax.optimization_barrier((part, second))
    pieces = [(sibling, (1, 1)), (first, (2, 4)), (first_sibling, (5, 3))]
    part, mark = score(part, pieces, False)
    second, early, part, _ = lax.optimization_barrier((second, early, part, mark))
    second_sibling = swap(second, "row", n, 1)
    early_sibling = swap(early, "row", n, 1)
    late, early_sibling = lax.optimization_barrier((late, early_sibling))
    corner = jnp.concatenate([early, late], axis=0)
    corner_sibling = jnp.concatenate([early_sibling, swap(late, "row", n, 1)], axis=0)
    pieces = [(second, (4, 2)), (second_sibling, (3, 5)), (corner, (6, 6)), (corner_sibling, (7, 7))]
    return [*score(part, pieces, True), names]


def on_device(n_row, n_col, source, target, source_mass, target_mass, tile_index, tile_count):
    tiles = source.shape[0] // TILE
    col_tiles = target.shape[0] // TILE
    slots = tile_index.shape[1]
    scale = LOG2_E / math.sqrt(source.shape[1])
    pairs = tiles * slots * TILE * TILE
    grid = (tiles, slots, TILE, TILE)
    source_rows, target_rows = (tiles, TILE), (col_tiles, TILE)
    a = source_mass.reshape(-1, LANES)
    b = target_mass.reshape(-1, LANES)
    index, count = tile_index.T, tile_count.T
    slot_rows = (tiles * slots, TILE)
    columns = (TILE, LANES)
    sizes = (n_row, n_col)

    def score(before, pieces, last):
        operands = [index, count, source, *[piece for piece, _ in pieces]]
        outs = [grid]
        if last:
            outs.append((2, *source_rows))
        if before is None:
            outs.append(slot_rows)
        else:
            operands.append(before)
            if not last:
                outs.append((8, LANES))
        distances = [k for _, k in pieces]
        return kernel_call(
            functools.partial(score_kernel, distances, before is None, last, scale),
            outs,
            operands,
            [columns],
            f"score_{len(pieces)}_{last}",
        )

    if n_row == 8 and target.shape[1] % LANES == 0:
        scores, stats, names = scores_by_chip(score, target, n_row)
    else:
        whole = lax.all_gather(target, "row", axis=1, tiled=True)
        scores, stats, names = score(None, [(whole, (0, 0))], True)

    def phase(body, name, outs, operands, parts, scratch=(), final=False, aliases=None):
        body = functools.partial(body, len(parts))
        return kernel_call(body, outs, [*operands, *parts], scratch, name, final, aliases)

    def added(values):
        return functools.reduce(jnp.add, values)

    flat = (tiles * TILE // LANES, LANES)
    parts = exchange(stats, "col", sizes, merged, ((1, 2), (3, 1), (2, 3)))
    (kernel,) = kernel_call(exp_kernel, [grid], [scores, stats], [columns], "exps")
    kernel, stats, tops, f_first, factor = phase(
        first_column_kernel,
        "column_0",
        [grid, (2, *target_rows), slot_rows, source_rows, source_rows],
        [names, scores, kernel, a],
        parts,
        [columns, slot_rows],
        aliases={2: 0},
    )
    parts = exchange(stats, "row", sizes, merged)
    sums, g_first, weights = phase(
        first_row_kernel,
        "row_1",
        [source_rows, target_rows, slot_rows],
        [names, kernel, b, factor, tops],
        parts,
        [columns],
    )
    parts = exchange(sums, "col", sizes, added)
    (sums,) = phase(
        lambda n, *refs: column_kernel(n, False, *refs),
        "column_1",
        [target_rows],
        [names, kernel, a, factor, weights],
        parts,
        [columns, slot_rows],
    )
    parts = exchange(sums, "row", sizes, added)
    (sums,) = phase(
        row_kernel,
        "row_2",
        [source_rows],
        [names, kernel, b, factor, weights],
        parts,
        [columns, slot_rows],
    )
    parts = exchange(sums, "col", sizes, added)
    sums, f_last = phase(
        lambda n, *refs: column_kernel(n, True, *refs),
        "column_2",
        [target_rows, flat],
        [names, kernel, a, factor, weights, f_first],
        parts,
        [columns, slot_rows],
    )
    parts = exchange(sums, "row", sizes, added)
    (g_last,) = phase(
        last_kernel, "last", [(col_tiles * TILE // LANES, LANES)], [b, g_first], parts, final=True
    )
    return (f_last.reshape(-1), g_last.reshape(-1))


def solution(mesh):
    placed = (P("row", None), P("col", "row"), P("row"), P("col"), P("row", "col"), P("row", "col"))
    return jax.shard_map(
        functools.partial(on_device, mesh.shape["row"], mesh.shape["col"]),
        mesh=mesh,
        in_specs=placed,
        out_specs=(P("row"), P("col")),
        check_vma=False,
    )
```

```python
import functools
import math

import jax
import jax.numpy as jnp
from jax import lax
from jax.experimental import pallas as pl
from jax.experimental.pallas import tpu as pltpu
from jax.sharding import PartitionSpec as P

TILE = 256
LANES = 128
STRIP = 32
FINE = 16
HALF = 64
LOW = -1e30
FLOOR = -1e29
LEAST = 1e-15
LOG2_E = math.log2(math.e)
LN_2 = math.log(2.0)

VMEM = pltpu.MemorySpace.VMEM
SMEM = pltpu.MemorySpace.SMEM
NT = (((1,), (1,)), ((), ()))


def kernel_call(body, outs, operands, scratch, name, final=False, aliases=None):
    specs = []
    placed = []
    for x in operands:
        if x.dtype == jnp.int32:
            specs.append(pl.BlockSpec(memory_space=SMEM))
            placed.append(x)
        else:
            specs.append(pl.BlockSpec(memory_space=VMEM))
            placed.append(pltpu.with_memory_space_constraint(x, VMEM))
    return pl.pallas_call(
        body,
        out_shape=[
            (jax.ShapeDtypeStruct if final else VMEM)(shape, jnp.float32) for shape in outs
        ],
        in_specs=specs,
        out_specs=[pl.BlockSpec(memory_space=VMEM)] * len(outs),
        input_output_aliases=aliases or {},
        scratch_shapes=[pltpu.VMEM(shape, jnp.float32) for shape in scratch],
        cost_estimate=pl.CostEstimate(flops=1 << 13, bytes_accessed=1 << 10, transcendentals=0),
        compiler_params=pltpu.CompilerParams(vmem_limit_bytes=8 << 20),
        name=name,
    )(*placed)


def to_rows(columns, tiles):
    return columns.T[:tiles]


def to_columns(rows):
    tiles = rows.shape[0]
    padded = jnp.concatenate([rows, jnp.zeros((LANES - tiles, TILE), jnp.float32)], axis=0)
    return padded.T


def put_lanes(ref, start, columns):
    size = next(iter(columns.values())).shape[0]
    rows = pl.ds(start, size)
    lane = lax.broadcasted_iota(jnp.int32, (size, LANES), 1)
    value = ref[rows, :]
    for at, column in columns.items():
        value = jnp.where(lane == at, column, value)
    ref[rows, :] = value


def halves(x, op):
    return op(x[:, :LANES], x[:, LANES:])


def from_flat(ref):
    step = TILE // LANES
    parts = [ref[pl.ds(h, ref.shape[0] // step, stride=step), :] for h in range(step)]
    return jnp.concatenate(parts, axis=1)


def put_flat(ref, value):
    for h in range(TILE // LANES):
        ref[pl.ds(h, value.shape[0], stride=TILE // LANES), :] = value[:, h * LANES : (h + 1) * LANES]


def score_kernel(distances, first, last, scale, *refs):
    pieces = len(distances)
    index, count, source = refs[:3]
    targets = refs[3 : 3 + pieces]
    refs = refs[3 + pieces :]
    if not first:
        before, *refs = refs
    score, *outs, columns = refs
    tiles, slots = score.shape[:2]
    me = lax.axis_index("row")
    offset = [
        (me ^ jnp.where((me & 1) == 0, zero, one)) * target.shape[1]
        for (zero, one), target in zip(distances, targets)
    ]
    if targets[0].shape[1] == source.shape[1]:
        offset = [0]
    if first:
        name_slots(index, count, outs[-1], slots)

    def products(t):
        rows = pl.ds(t * TILE if last else pl.multiple_of(t * TILE, TILE), TILE)
        left = [
            source[rows, pl.ds(pl.multiple_of(offset[k], targets[k].shape[1]), targets[k].shape[1])]
            for k in range(pieces)
        ]
        left = jnp.concatenate(left, axis=1) if pieces > 1 else left[0]
        for s in range(slots):
            chosen = pl.ds(pl.multiple_of(index[s, t] * TILE, TILE), TILE)
            right = [targets[k][chosen, :] for k in range(pieces)]
            right = jnp.concatenate(right, axis=1) if pieces > 1 else right[0]
            block = lax.dot_general(left, right, NT, preferred_element_type=jnp.float32)
            if not first:
                block = before[t, s] + block
            if last:
                block = block * scale
                if s > 0:
                    block = jnp.where(s < count[0, t], block, LOW)
            score[t, s] = block

    def statistics(t):
        for r in range(0, TILE, FINE):
            blocks = [score[t, s, r : r + FINE] for s in range(slots)]
            top = halves(functools.reduce(jnp.maximum, blocks), jnp.maximum)
            top = jnp.max(top, axis=1, keepdims=True)
            total = functools.reduce(jnp.add, [jnp.exp2(block - top) for block in blocks])
            total = jnp.sum(halves(total, jnp.add), axis=1, keepdims=True)
            put_lanes(columns, r, {t: top, HALF + t: total})

    if last:
        for t in range(tiles + 1):
            if t < tiles:
                products(t)
            if t > 0:
                statistics(t - 1)
        stats = columns[...].T
        outs[0][0] = stats[:tiles]
        outs[0][1] = stats[HALF : HALF + tiles]
    else:
        lax.fori_loop(0, tiles, lambda t, carry: (products(t), carry)[1], 0, unroll=4)
    if not first and not last:
        outs[0][...] = jnp.zeros(outs[0].shape, jnp.float32)


def name_slots(index, count, names, slots):
    for k in range(names.shape[0]):
        t, s = divmod(k, slots)
        name = jnp.where(s < count[0, t], index[s, t], -1).astype(jnp.float32)
        names[k : k + 1, :] = jnp.full((1, TILE), name, jnp.float32)


def to_slots(names, rows):
    taken = jnp.zeros(names.shape, jnp.float32)
    for u in range(rows.shape[0]):
        taken = jnp.where(names == u, rows[u : u + 1, :], taken)
    return taken


def to_targets(names, values, out, op, empty):
    for u in range(out.shape[0]):
        out[u : u + 1, :] = op(jnp.where(names == u, values, empty), axis=0, keepdims=True)


def merge(refs):
    top = functools.reduce(jnp.maximum, [ref[0] for ref in refs])
    total = functools.reduce(jnp.add, [ref[1] * jnp.exp2(ref[0] - top) for ref in refs])
    return top, total


def total_of(refs):
    return functools.reduce(jnp.add, [ref[...] for ref in refs])


def exp_kernel(score, stats, kernel, columns):
    tiles, slots = kernel.shape[:2]
    columns[...] = to_columns(stats[0])
    for t in range(tiles):
        for r in range(0, TILE, STRIP):
            column = columns[r : r + STRIP, t : t + 1]
            for s in range(slots):
                kernel[t, s, r : r + STRIP] = jnp.exp2(score[t, s, r : r + STRIP] - column)


def slot_sums(kernel, columns, sums):
    tiles, slots = kernel.shape[:2]
    for t in range(tiles):
        total = [None] * slots
        for r in range(0, TILE, STRIP):
            column = columns[r : r + STRIP, t : t + 1]
            for s in range(slots):
                block = kernel[t, s, r : r + STRIP] * column
                total[s] = block if r == 0 else total[s] + block
        for s in range(slots):
            k = t * slots + s
            sums[k : k + 1, :] = jnp.sum(total[s], axis=0, keepdims=True)


def first_column_kernel(parts, names, score, before, mass, *refs):
    gathered = refs[:parts]
    kernel, stats, tops, potential, factor, columns, sums = refs[parts:]
    tiles, slots = kernel.shape[:2]
    top, total = merge(gathered)
    row = LOG2_E * (jnp.log(from_flat(mass)) - jnp.log(total)) - top
    potential[...] = row
    factor[...] = jnp.exp2(gathered[0][0] + row)
    columns[...] = to_columns(factor[...])
    slot_sums(before, columns, sums)
    named = names[...]
    tops[...] = jnp.zeros(tops.shape, jnp.float32)
    to_targets(named, sums[...], stats.at[1], jnp.sum, 0.0)
    stats[0] = jnp.where(stats[1] > 0.0, 0.0, FLOOR)
    least = jnp.min(jnp.where(named >= 0, sums[...], 1.0))

    @pl.when(least < LEAST)
    def _():
        factor[...] = jnp.ones(factor.shape, jnp.float32)
        columns[...] = to_columns(row)
        for t in range(tiles):
            best = [None] * slots
            for r in range(0, TILE, STRIP):
                column = columns[r : r + STRIP, t : t + 1]
                for s in range(slots):
                    block = score[t, s, r : r + STRIP] + column
                    best[s] = block if r == 0 else jnp.maximum(best[s], block)
            best = [jnp.maximum(jnp.max(x, axis=0, keepdims=True), FLOOR) for x in best]
            total = [None] * slots
            for r in range(0, TILE, STRIP):
                column = columns[r : r + STRIP, t : t + 1]
                for s in range(slots):
                    block = jnp.exp2(score[t, s, r : r + STRIP] + column - best[s])
                    kernel[t, s, r : r + STRIP] = block
                    total[s] = block if r == 0 else total[s] + block
            for s in range(slots):
                k = t * slots + s
                tops[k : k + 1, :] = best[s]
                sums[k : k + 1, :] = jnp.sum(total[s], axis=0, keepdims=True)
        to_targets(named, tops[...], stats.at[0], jnp.max, FLOOR)
        change = jnp.exp2(tops[...] - to_slots(named, stats[0]))
        to_targets(named, sums[...] * change, stats.at[1], jnp.sum, 0.0)


def row_sums(kernel, weights, factor, out, columns):
    tiles, slots = kernel.shape[:2]
    for t in range(tiles):
        weight = [weights[t * slots + s : t * slots + s + 1, :] for s in range(slots)]
        for r in range(0, TILE, STRIP):
            blocks = [kernel[t, s, r : r + STRIP] * weight[s] for s in range(slots)]
            total = halves(functools.reduce(jnp.add, blocks), jnp.add)
            put_lanes(columns, r, {t: jnp.sum(total, axis=1, keepdims=True)})
    out[...] = to_rows(columns[...], tiles) * factor[...]


def first_row_kernel(parts, names, kernel, mass, factor, tops, *refs):
    gathered = refs[:parts]
    out, potential, weights, columns = refs[parts:]
    top, total = merge(gathered)
    value = LOG2_E * (jnp.log(from_flat(mass)) - jnp.log(total)) - top
    potential[...] = value
    weights[...] = jnp.exp2(tops[...] + to_slots(names[...], value))
    row_sums(kernel, weights, factor, out, columns)


def column_kernel(parts, last, names, kernel, mass, factor, weights, *refs):
    if last:
        start, *refs = refs
    gathered = refs[:parts]
    out, *potential, columns, sums = refs[parts:]
    scaling = from_flat(mass) / total_of(gathered)
    columns[...] = to_columns(scaling * factor[...])
    slot_sums(kernel, columns, sums)
    to_targets(names[...], sums[...] * weights[...], out, jnp.sum, 0.0)
    if last:
        put_flat(potential[0], LN_2 * start[...] + jnp.log(scaling))


def row_kernel(parts, names, kernel, mass, factor, weights, *refs):
    gathered = refs[:parts]
    out, columns, scaled = refs[parts:]
    scaling = from_flat(mass) / total_of(gathered)
    scaled[...] = weights[...] * to_slots(names[...], scaling)
    row_sums(kernel, scaled, factor, out, columns)


def last_kernel(parts, mass, start, *refs):
    scaling = from_flat(mass) / total_of(refs[:parts])
    put_flat(refs[parts], LN_2 * start[...] + jnp.log(scaling))


def permute(x, axis, n, partner):
    return lax.ppermute(x, axis, [(i, partner(i)) for i in range(n)])


def swap(x, axis, n, mask):
    return permute(x, axis, n, lambda i: i ^ mask)


def merged(pairs):
    top = functools.reduce(jnp.maximum, [pair[0] for pair in pairs])
    total = functools.reduce(jnp.add, [pair[1] * jnp.exp2(pair[0] - top) for pair in pairs])
    here = lax.broadcasted_iota(jnp.int32, pairs[0].shape, 0)
    return jnp.where(here == 0, top[None], total[None])


def exchange(x, axis, sizes, join, orders=((3, 1), (2, 3), (1, 2))):
    n = sizes[axis]
    if n & (n - 1):
        return [lax.all_gather(x, axis)[k] for k in range(n)]
    low, pairwise = 1, []
    while n // low not in (1, 4):
        pairwise.append(low)
        low *= 2
    mixed = axis == "col" or low > 1
    parts = [x]
    for even, odd in orders if low < n else ():
        pairs = []
        for row in range(sizes["row"]):
            for col in range(sizes["col"]):
                mask = low * (odd if mixed and row & 1 else even)
                to = (row ^ mask, col) if axis == "row" else (row, col ^ mask)
                pairs.append((row * sizes["col"] + col, to[0] * sizes["col"] + to[1]))
        parts.append(lax.ppermute(x, ("row", "col"), pairs))
    for mask in pairwise:
        x = join(parts)
        parts = [x, swap(x, axis, n, mask)]
    return parts


def first_way(i):
    return i ^ (4 if i & 1 else 2)


def second_way(i):
    return i ^ (2 if i & 1 else 4)


def scores_by_chip(score, target, n):
    first = permute(target, "row", n, first_way)
    part, names = score(None, [(target, (0, 0))], False)
    later, names = lax.optimization_barrier((target, names))
    second = permute(later, "row", n, second_way)
    first, part, names = lax.optimization_barrier((first, part, names))
    cut = first.shape[0] // 2
    early, late = (permute(part, "row", n, second_way) for part in (first[:cut], first[cut:]))
    sibling = swap(target, "row", n, 1)
    first_sibling = swap(first, "row", n, 1)
    part, second = lax.optimization_barrier((part, second))
    pieces = [(sibling, (1, 1)), (first, (2, 4)), (first_sibling, (5, 3))]
    part, mark = score(part, pieces, False)
    second, early, part, _ = lax.optimization_barrier((second, early, part, mark))
    second_sibling = swap(second, "row", n, 1)
    early_sibling = swap(early, "row", n, 1)
    late, early_sibling = lax.optimization_barrier((late, early_sibling))
    corner = jnp.concatenate([early, late], axis=0)
    corner_sibling = jnp.concatenate([early_sibling, swap(late, "row", n, 1)], axis=0)
    pieces = [(second, (4, 2)), (second_sibling, (3, 5)), (corner, (6, 6)), (corner_sibling, (7, 7))]
    return [*score(part, pieces, True), names]


def on_device(n_row, n_col, source, target, source_mass, target_mass, tile_index, tile_count):
    tiles = source.shape[0] // TILE
    col_tiles = target.shape[0] // TILE
    slots = tile_index.shape[1]
    scale = LOG2_E / math.sqrt(source.shape[1])
    pairs = tiles * slots * TILE * TILE
    grid = (tiles, slots, TILE, TILE)
    source_rows, target_rows = (tiles, TILE), (col_tiles, TILE)
    a = source_mass.reshape(-1, LANES)
    b = target_mass.reshape(-1, LANES)
    index, count = tile_index.T, tile_count.T
    slot_rows = (tiles * slots, TILE)
    columns = (TILE, LANES)
    sizes = {"row": n_row, "col": n_col}

    def score(before, pieces, last):
        operands = [index, count, source, *[piece for piece, _ in pieces]]
        outs = [grid]
        if last:
            outs.append((2, *source_rows))
        if before is None:
            outs.append(slot_rows)
        else:
            operands.append(before)
            if not last:
                outs.append((8, LANES))
        distances = [k for _, k in pieces]
        return kernel_call(
            functools.partial(score_kernel, distances, before is None, last, scale),
            outs,
            operands,
            [columns],
            f"score_{len(pieces)}_{last}",
        )

    if n_row == 8 and target.shape[1] % LANES == 0:
        scores, stats, names = scores_by_chip(score, target, n_row)
    else:
        whole = lax.all_gather(target, "row", axis=1, tiled=True)
        scores, stats, names = score(None, [(whole, (0, 0))], True)

    def phase(body, name, outs, operands, parts, scratch=(), final=False, aliases=None):
        body = functools.partial(body, len(parts))
        return kernel_call(body, outs, [*operands, *parts], scratch, name, final, aliases)

    def added(values):
        return functools.reduce(jnp.add, values)

    flat = (tiles * TILE // LANES, LANES)
    parts = exchange(stats, "col", sizes, merged, ((1, 2), (3, 1), (2, 3)))
    (kernel,) = kernel_call(exp_kernel, [grid], [scores, stats], [columns], "exps")
    kernel, stats, tops, f_first, factor = phase(
        first_column_kernel,
        "column_0",
        [grid, (2, *target_rows), slot_rows, source_rows, source_rows],
        [names, scores, kernel, a],
        parts,
        [columns, slot_rows],
        aliases={2: 0},
    )
    parts = exchange(stats, "row", sizes, merged)
    sums, g_first, weights = phase(
        first_row_kernel,
        "row_1",
        [source_rows, target_rows, slot_rows],
        [names, kernel, b, factor, tops],
        parts,
        [columns],
    )
    parts = exchange(sums, "col", sizes, added)
    (sums,) = phase(
        lambda n, *refs: column_kernel(n, False, *refs),
        "column_1",
        [target_rows],
        [names, kernel, a, factor, weights],
        parts,
        [columns, slot_rows],
    )
    parts = exchange(sums, "row", sizes, added)
    (sums,) = phase(
        row_kernel,
        "row_2",
        [source_rows],
        [names, kernel, b, factor, weights],
        parts,
        [columns, slot_rows],
    )
    parts = exchange(sums, "col", sizes, added)
    sums, f_last = phase(
        lambda n, *refs: column_kernel(n, True, *refs),
        "column_2",
        [target_rows, flat],
        [names, kernel, a, factor, weights, f_first],
        parts,
        [columns, slot_rows],
    )
    parts = exchange(sums, "row", sizes, added)
    (g_last,) = phase(
        last_kernel, "last", [(col_tiles * TILE // LANES, LANES)], [b, g_first], parts, final=True
    )
    return (f_last.reshape(-1), g_last.reshape(-1))


def solution(mesh):
    placed = (P("row", None), P("col", "row"), P("row"), P("col"), P("row", "col"), P("row", "col"))
    return jax.shard_map(
        functools.partial(on_device, mesh.shape["row"], mesh.shape["col"]),
        mesh=mesh,
        in_specs=placed,
        out_specs=(P("row"), P("col")),
        check_vma=False,
    )
```

```python
import functools
import math

import jax
import jax.numpy as jnp
from jax import lax
from jax.experimental import pallas as pl
from jax.experimental.pallas import tpu as pltpu
from jax.sharding import PartitionSpec as P

TILE = 256
LANES = 128
STRIP = 16
FINE = 32
HALF = 64
LOW = -1e30
FLOOR = -1e29
LEAST = 1e-15
LOG2_E = math.log2(math.e)
LN_2 = math.log(2.0)

VMEM = pltpu.MemorySpace.VMEM
SMEM = pltpu.MemorySpace.SMEM
NT = (((1,), (1,)), ((), ()))


def kernel_call(body, outs, operands, scratch, name, final=False, aliases=None):
    specs = []
    placed = []
    for x in operands:
        if x.dtype == jnp.int32:
            specs.append(pl.BlockSpec(memory_space=SMEM))
            placed.append(x)
        else:
            specs.append(pl.BlockSpec(memory_space=VMEM))
            placed.append(pltpu.with_memory_space_constraint(x, VMEM))
    return pl.pallas_call(
        body,
        out_shape=[
            (jax.ShapeDtypeStruct if final else VMEM)(shape, jnp.float32) for shape in outs
        ],
        in_specs=specs,
        out_specs=[pl.BlockSpec(memory_space=VMEM)] * len(outs),
        input_output_aliases=aliases or {},
        scratch_shapes=[pltpu.VMEM(shape, jnp.float32) for shape in scratch],
        cost_estimate=pl.CostEstimate(flops=1 << 13, bytes_accessed=1 << 10, transcendentals=0),
        compiler_params=pltpu.CompilerParams(vmem_limit_bytes=8 << 20),
        name=name,
    )(*placed)


def to_rows(columns, tiles):
    return columns.T[:tiles]


def to_columns(rows):
    tiles = rows.shape[0]
    padded = jnp.concatenate([rows, jnp.zeros((LANES - tiles, TILE), jnp.float32)], axis=0)
    return padded.T


def put_lanes(ref, start, columns):
    size = next(iter(columns.values())).shape[0]
    rows = pl.ds(start, size)
    lane = lax.broadcasted_iota(jnp.int32, (size, LANES), 1)
    value = ref[rows, :]
    for at, column in columns.items():
        value = jnp.where(lane == at, column, value)
    ref[rows, :] = value


def halves(x, op):
    return op(x[:, :LANES], x[:, LANES:])


def from_flat(ref):
    step = TILE // LANES
    parts = [ref[pl.ds(h, ref.shape[0] // step, stride=step), :] for h in range(step)]
    return jnp.concatenate(parts, axis=1)


def put_flat(ref, value):
    for h in range(TILE // LANES):
        ref[pl.ds(h, value.shape[0], stride=TILE // LANES), :] = value[:, h * LANES : (h + 1) * LANES]


def score_kernel(distances, first, last, scale, *refs):
    pieces = len(distances)
    index, count, source = refs[:3]
    targets = refs[3 : 3 + pieces]
    refs = refs[3 + pieces :]
    if not first:
        before, *refs = refs
    score, *outs, columns = refs
    tiles, slots = score.shape[:2]
    me = lax.axis_index("row")
    offset = [
        (me ^ jnp.where((me & 1) == 0, zero, one)) * target.shape[1]
        for (zero, one), target in zip(distances, targets)
    ]
    if targets[0].shape[1] == source.shape[1]:
        offset = [0]
    if first:
        name_slots(index, count, outs[-1], slots)

    def products(t):
        rows = pl.ds(t * TILE if last else pl.multiple_of(t * TILE, TILE), TILE)
        left = [
            source[rows, pl.ds(pl.multiple_of(offset[k], targets[k].shape[1]), targets[k].shape[1])]
            for k in range(pieces)
        ]
        left = jnp.concatenate(left, axis=1) if pieces > 1 else left[0]
        for s in range(slots):
            chosen = pl.ds(pl.multiple_of(index[s, t] * TILE, TILE), TILE)
            right = [targets[k][chosen, :] for k in range(pieces)]
            right = jnp.concatenate(right, axis=1) if pieces > 1 else right[0]
            block = lax.dot_general(left, right, NT, preferred_element_type=jnp.float32)
            if not first:
                block = before[t, s] + block
            if last:
                block = block * scale
                if s > 0:
                    block = jnp.where(s < count[0, t], block, LOW)
            score[t, s] = block

    def statistics(t):
        for r in range(0, TILE, FINE):
            blocks = [score[t, s, r : r + FINE] for s in range(slots)]
            top = halves(functools.reduce(jnp.maximum, blocks), jnp.maximum)
            top = jnp.max(top, axis=1, keepdims=True)
            total = functools.reduce(jnp.add, [jnp.exp2(block - top) for block in blocks])
            total = jnp.sum(halves(total, jnp.add), axis=1, keepdims=True)
            put_lanes(columns, r, {t: top, HALF + t: total})

    if last:
        for t in range(tiles + 1):
            if t < tiles:
                products(t)
            if t > 0:
                statistics(t - 1)
        stats = columns[...].T
        outs[0][0] = stats[:tiles]
        outs[0][1] = stats[HALF : HALF + tiles]
    else:
        lax.fori_loop(0, tiles, lambda t, carry: (products(t), carry)[1], 0, unroll=4)
    if not first and not last:
        outs[0][...] = jnp.zeros(outs[0].shape, jnp.float32)


def name_slots(index, count, names, slots):
    for k in range(names.shape[0]):
        t, s = divmod(k, slots)
        name = jnp.where(s < count[0, t], index[s, t], -1).astype(jnp.float32)
        names[k : k + 1, :] = jnp.full((1, TILE), name, jnp.float32)


def to_slots(names, rows):
    taken = jnp.zeros(names.shape, jnp.float32)
    for u in range(rows.shape[0]):
        taken = jnp.where(names == u, rows[u : u + 1, :], taken)
    return taken


def to_targets(names, values, out, op, empty):
    for u in range(out.shape[0]):
        out[u : u + 1, :] = op(jnp.where(names == u, values, empty), axis=0, keepdims=True)


def merge(refs):
    top = functools.reduce(jnp.maximum, [ref[0] for ref in refs])
    total = functools.reduce(jnp.add, [ref[1] * jnp.exp2(ref[0] - top) for ref in refs])
    return top, total


def total_of(refs):
    return functools.reduce(jnp.add, [ref[...] for ref in refs])


def exp_kernel(score, stats, kernel, columns):
    tiles, slots = kernel.shape[:2]
    columns[...] = to_columns(stats[0])
    for t in range(tiles):
        for r in range(0, TILE, STRIP):
            column = columns[r : r + STRIP, t : t + 1]
            for s in range(slots):
                kernel[t, s, r : r + STRIP] = jnp.exp2(score[t, s, r : r + STRIP] - column)


def slot_sums(kernel, columns, sums):
    tiles, slots = kernel.shape[:2]
    for t in range(tiles):
        total = [None] * slots
        for r in range(0, TILE, STRIP):
            column = columns[r : r + STRIP, t : t + 1]
            for s in range(slots):
                block = kernel[t, s, r : r + STRIP] * column
                total[s] = block if r == 0 else total[s] + block
        for s in range(slots):
            k = t * slots + s
            sums[k : k + 1, :] = jnp.sum(total[s], axis=0, keepdims=True)


def first_column_kernel(parts, names, score, before, mass, *refs):
    gathered = refs[:parts]
    kernel, stats, tops, potential, factor, columns, sums = refs[parts:]
    tiles, slots = kernel.shape[:2]
    top, total = merge(gathered)
    row = LOG2_E * (jnp.log(from_flat(mass)) - jnp.log(total)) - top
    potential[...] = row
    factor[...] = jnp.exp2(gathered[0][0] + row)
    columns[...] = to_columns(factor[...])
    slot_sums(before, columns, sums)
    named = names[...]
    tops[...] = jnp.zeros(tops.shape, jnp.float32)
    to_targets(named, sums[...], stats.at[1], jnp.sum, 0.0)
    stats[0] = jnp.where(stats[1] > 0.0, 0.0, FLOOR)
    least = jnp.min(jnp.where(named >= 0, sums[...], 1.0))

    @pl.when(least < LEAST)
    def _():
        factor[...] = jnp.ones(factor.shape, jnp.float32)
        columns[...] = to_columns(row)
        for t in range(tiles):
            best = [None] * slots
            for r in range(0, TILE, STRIP):
                column = columns[r : r + STRIP, t : t + 1]
                for s in range(slots):
                    block = score[t, s, r : r + STRIP] + column
                    best[s] = block if r == 0 else jnp.maximum(best[s], block)
            best = [jnp.maximum(jnp.max(x, axis=0, keepdims=True), FLOOR) for x in best]
            total = [None] * slots
            for r in range(0, TILE, STRIP):
                column = columns[r : r + STRIP, t : t + 1]
                for s in range(slots):
                    block = jnp.exp2(score[t, s, r : r + STRIP] + column - best[s])
                    kernel[t, s, r : r + STRIP] = block
                    total[s] = block if r == 0 else total[s] + block
            for s in range(slots):
                k = t * slots + s
                tops[k : k + 1, :] = best[s]
                sums[k : k + 1, :] = jnp.sum(total[s], axis=0, keepdims=True)
        to_targets(named, tops[...], stats.at[0], jnp.max, FLOOR)
        change = jnp.exp2(tops[...] - to_slots(named, stats[0]))
        to_targets(named, sums[...] * change, stats.at[1], jnp.sum, 0.0)


def row_sums(kernel, weights, factor, out, columns):
    tiles, slots = kernel.shape[:2]
    for t in range(tiles):
        weight = [weights[t * slots + s : t * slots + s + 1, :] for s in range(slots)]
        for r in range(0, TILE, STRIP):
            blocks = [kernel[t, s, r : r + STRIP] * weight[s] for s in range(slots)]
            total = halves(functools.reduce(jnp.add, blocks), jnp.add)
            put_lanes(columns, r, {t: jnp.sum(total, axis=1, keepdims=True)})
    out[...] = to_rows(columns[...], tiles) * factor[...]


def first_row_kernel(parts, names, kernel, mass, factor, tops, *refs):
    gathered = refs[:parts]
    out, potential, weights, columns = refs[parts:]
    top, total = merge(gathered)
    value = LOG2_E * (jnp.log(from_flat(mass)) - jnp.log(total)) - top
    potential[...] = value
    weights[...] = jnp.exp2(tops[...] + to_slots(names[...], value))
    row_sums(kernel, weights, factor, out, columns)


def column_kernel(parts, last, names, kernel, mass, factor, weights, *refs):
    if last:
        start, *refs = refs
    gathered = refs[:parts]
    out, *potential, columns, sums = refs[parts:]
    scaling = from_flat(mass) / total_of(gathered)
    columns[...] = to_columns(scaling * factor[...])
    slot_sums(kernel, columns, sums)
    to_targets(names[...], sums[...] * weights[...], out, jnp.sum, 0.0)
    if last:
        put_flat(potential[0], LN_2 * start[...] + jnp.log(scaling))


def row_kernel(parts, names, kernel, mass, factor, weights, *refs):
    gathered = refs[:parts]
    out, columns, scaled = refs[parts:]
    scaling = from_flat(mass) / total_of(gathered)
    scaled[...] = weights[...] * to_slots(names[...], scaling)
    row_sums(kernel, scaled, factor, out, columns)


def last_kernel(parts, mass, start, *refs):
    scaling = from_flat(mass) / total_of(refs[:parts])
    put_flat(refs[parts], LN_2 * start[...] + jnp.log(scaling))


def permute(x, axis, n, partner):
    return lax.ppermute(x, axis, [(i, partner(i)) for i in range(n)])


def swap(x, axis, n, mask):
    return permute(x, axis, n, lambda i: i ^ mask)


def merged(pairs):
    top = functools.reduce(jnp.maximum, [pair[0] for pair in pairs])
    total = functools.reduce(jnp.add, [pair[1] * jnp.exp2(pair[0] - top) for pair in pairs])
    here = lax.broadcasted_iota(jnp.int32, pairs[0].shape, 0)
    return jnp.where(here == 0, top[None], total[None])


def exchange(x, axis, sizes, join, orders=((3, 1), (2, 3), (1, 2))):
    n = sizes[axis]
    if n & (n - 1):
        return [lax.all_gather(x, axis)[k] for k in range(n)]
    low, pairwise = 1, []
    while n // low not in (1, 4):
        pairwise.append(low)
        low *= 2
    mixed = axis == "col" or low > 1
    parts = [x]
    for even, odd in orders if low < n else ():
        pairs = []
        for row in range(sizes["row"]):
            for col in range(sizes["col"]):
                mask = low * (odd if mixed and row & 1 else even)
                to = (row ^ mask, col) if axis == "row" else (row, col ^ mask)
                pairs.append((row * sizes["col"] + col, to[0] * sizes["col"] + to[1]))
        parts.append(lax.ppermute(x, ("row", "col"), pairs))
    for mask in pairwise:
        x = join(parts)
        parts = [x, swap(x, axis, n, mask)]
    return parts


def first_way(i):
    return i ^ (4 if i & 1 else 2)


def second_way(i):
    return i ^ (2 if i & 1 else 4)


def scores_by_chip(score, target, n):
    first = permute(target, "row", n, first_way)
    part, names = score(None, [(target, (0, 0))], False)
    later, names = lax.optimization_barrier((target, names))
    second = permute(later, "row", n, second_way)
    first, part, names = lax.optimization_barrier((first, part, names))
    cut = first.shape[0] // 2
    early, late = (permute(part, "row", n, second_way) for part in (first[:cut], first[cut:]))
    sibling = swap(target, "row", n, 1)
    first_sibling = swap(first, "row", n, 1)
    part, second = lax.optimization_barrier((part, second))
    pieces = [(sibling, (1, 1)), (first, (2, 4)), (first_sibling, (5, 3))]
    part, mark = score(part, pieces, False)
    second, early, part, _ = lax.optimization_barrier((second, early, part, mark))
    second_sibling = swap(second, "row", n, 1)
    early_sibling = swap(early, "row", n, 1)
    late, early_sibling = lax.optimization_barrier((late, early_sibling))
    corner = jnp.concatenate([early, late], axis=0)
    corner_sibling = jnp.concatenate([early_sibling, swap(late, "row", n, 1)], axis=0)
    pieces = [(second, (4, 2)), (second_sibling, (3, 5)), (corner, (6, 6)), (corner_sibling, (7, 7))]
    return [*score(part, pieces, True), names]


def on_device(n_row, n_col, source, target, source_mass, target_mass, tile_index, tile_count):
    tiles = source.shape[0] // TILE
    col_tiles = target.shape[0] // TILE
    slots = tile_index.shape[1]
    scale = LOG2_E / math.sqrt(source.shape[1])
    pairs = tiles * slots * TILE * TILE
    grid = (tiles, slots, TILE, TILE)
    source_rows, target_rows = (tiles, TILE), (col_tiles, TILE)
    a = source_mass.reshape(-1, LANES)
    b = target_mass.reshape(-1, LANES)
    index, count = tile_index.T, tile_count.T
    slot_rows = (tiles * slots, TILE)
    columns = (TILE, LANES)
    sizes = {"row": n_row, "col": n_col}

    def score(before, pieces, last):
        operands = [index, count, source, *[piece for piece, _ in pieces]]
        outs = [grid]
        if last:
            outs.append((2, *source_rows))
        if before is None:
            outs.append(slot_rows)
        else:
            operands.append(before)
            if not last:
                outs.append((8, LANES))
        distances = [k for _, k in pieces]
        return kernel_call(
            functools.partial(score_kernel, distances, before is None, last, scale),
            outs,
            operands,
            [columns],
            f"score_{len(pieces)}_{last}",
        )

    if n_row == 8 and target.shape[1] % LANES == 0:
        scores, stats, names = scores_by_chip(score, target, n_row)
    else:
        whole = lax.all_gather(target, "row", axis=1, tiled=True)
        scores, stats, names = score(None, [(whole, (0, 0))], True)

    def phase(body, name, outs, operands, parts, scratch=(), final=False, aliases=None):
        body = functools.partial(body, len(parts))
        return kernel_call(body, outs, [*operands, *parts], scratch, name, final, aliases)

    def added(values):
        return functools.reduce(jnp.add, values)

    flat = (tiles * TILE // LANES, LANES)
    parts = exchange(stats, "col", sizes, merged, ((1, 2), (3, 1), (2, 3)))
    (kernel,) = kernel_call(exp_kernel, [grid], [scores, stats], [columns], "exps")
    kernel, stats, tops, f_first, factor = phase(
        first_column_kernel,
        "column_0",
        [grid, (2, *target_rows), slot_rows, source_rows, source_rows],
        [names, scores, kernel, a],
        parts,
        [columns, slot_rows],
        aliases={2: 0},
    )
    parts = exchange(stats, "row", sizes, merged)
    sums, g_first, weights = phase(
        first_row_kernel,
        "row_1",
        [source_rows, target_rows, slot_rows],
        [names, kernel, b, factor, tops],
        parts,
        [columns],
    )
    parts = exchange(sums, "col", sizes, added)
    (sums,) = phase(
        lambda n, *refs: column_kernel(n, False, *refs),
        "column_1",
        [target_rows],
        [names, kernel, a, factor, weights],
        parts,
        [columns, slot_rows],
    )
    parts = exchange(sums, "row", sizes, added)
    (sums,) = phase(
        row_kernel,
        "row_2",
        [source_rows],
        [names, kernel, b, factor, weights],
        parts,
        [columns, slot_rows],
    )
    parts = exchange(sums, "col", sizes, added)
    sums, f_last = phase(
        lambda n, *refs: column_kernel(n, True, *refs),
        "column_2",
        [target_rows, flat],
        [names, kernel, a, factor, weights, f_first],
        parts,
        [columns, slot_rows],
    )
    parts = exchange(sums, "row", sizes, added)
    (g_last,) = phase(
        last_kernel, "last", [(col_tiles * TILE // LANES, LANES)], [b, g_first], parts, final=True
    )
    return (f_last.reshape(-1), g_last.reshape(-1))


def solution(mesh):
    placed = (P("row", None), P("col", "row"), P("row"), P("col"), P("row", "col"), P("row", "col"))
    return jax.shard_map(
        functools.partial(on_device, mesh.shape["row"], mesh.shape["col"]),
        mesh=mesh,
        in_specs=placed,
        out_specs=(P("row"), P("col")),
        check_vma=False,
    )
```
